32 devices in a mesh: groups: 2 (over y), fsdp: 4 (over z), dp: 2 (over x), pair: 2 (over core).
Axes of the slice: x: 2, y: 2, z: 4, core: 2. Of those that a mesh axis runs over, the one named last changes fastest.
Arguments:
- hidden_input: bfloat16 [4096, 8192], P(('groups', 'fsdp', 'dp', 'pair')), parts along dimension 0, may hold values from -6 to 6
- norm_gain_vector: float32 [8192], replicated, may hold values from 0.5 to 18, as said below
- value_matrix: bfloat16 [8192, 768], P('fsdp'), may hold values from -0.0625 to 0.0625
- adapter_down_map: bfloat16 [16384, 64], P(('groups', 'fsdp')), parts along dimension 0, may hold values from -0.0625 to 0.0625
- adapter_up_map: bfloat16 [128, 768], P('groups'), parts along dimension 0, may hold values from -5 to 5
- values_gradient: bfloat16 [4096, 768], P(('groups', 'fsdp', 'dp', 'pair')), parts along dimension 0, may hold values from -6 to 6
Outputs:
- grad_hidden: bfloat16 [4096, 8192], P(('groups', 'fsdp', 'dp', 'pair')), parts along dimension 0
- grad_down: float32 [16384, 64], P(('groups', 'fsdp')), parts along dimension 0
- grad_up: float32 [128, 768], P('groups'), parts along dimension 0
The draws below stay inside these ranges and needn't reach their ends.
There are 2 independent parts, one for each index of `groups`. The reference program is written for one: setup_inputs(seed, part) draws one part's arguments, and reference() takes and returns one part's arrays. A program takes and returns all parts, laid end to end along the dimension named above; an argument that names none is the same for every part. Nothing has to cross between parts.
Inputs may be any that keep to these rules, and one draw needn't show every extreme that they name: `norm_gain_vector`: positive gains.
All inputs are finite; a program needn't handle non-finite values.
Results may differ from the reference program's by a relative error of at most 0.0085.
Values may be sent and summed in bfloat16 or wider, within the bound.
A program may use at most 64 MiB of HBM per device.

```python
import math
import jax
import jax.numpy as jnp
from jax import lax

MODEL_WIDTH = 8192
ADAPTER_RANK = 64
KVW = 768
TOKENS = 2048


def draw_norm_gain_vector(key, part):
    key = jax.random.fold_in(key, 11)
    position = jnp.arange(MODEL_WIDTH, dtype=jnp.float32) / (MODEL_WIDTH - 1)
    noise = jax.random.uniform(key, (MODEL_WIDTH,), jnp.float32, -math.log(2.0), math.log(2.0))
    rising = 3.0
    return jnp.exp(position * math.log(rising) + noise)


def draw_adapter_up_map(key, part):
    key = jax.random.fold_in(key, 23)
    first_key, second_key = jax.random.split(key)
    lower, upper = (0.3, 3.0)
    row_scales = jnp.exp(jax.random.uniform(first_key, (ADAPTER_RANK, 1), jnp.float32, math.log(lower), math.log(upper)))
    entries = jnp.clip(jax.random.normal(second_key, (ADAPTER_RANK, KVW), jnp.float32), -5.0, 5.0) / math.sqrt(KVW)
    return (row_scales * entries).astype(jnp.bfloat16)


def with_spikes(array, key, source, target, shards_of, factor):
    owner, partner = [(jnp.arange(array.shape[dim]) // (array.shape[dim] // shards_of)).reshape([-1 if axis == dim else 1 for axis in range(array.ndim)]) for dim in (source, target)]
    chosen = jax.random.permutation(key, shards_of)[partner]
    strong = (owner == chosen) | (owner == (partner + shards_of // 2) % shards_of)
    return jnp.where(strong, factor * array, array)


def block_levels(own_key, dims, cuts, low, high):
    loudness = 1.0
    for axis_at, parts in cuts:
        heights = jax.random.uniform(jax.random.fold_in(jax.random.fold_in(own_key, 6), axis_at), (parts,), jnp.float32, low / len(cuts), high / len(cuts))
        loudness = loudness * jnp.repeat(jnp.exp(heights), dims[axis_at] // parts).reshape((-1,) + (1,) * (len(dims) - 1 - axis_at))
    return loudness


def bell_draw(key, dims, scale, reach, cuts=(), held_as=jnp.bfloat16):
    drawn = jax.random.normal(key, dims, jnp.float32) * scale
    if len(cuts) > 0:
        drawn = block_levels(key, dims, cuts, -0.22, 0.18) * drawn
    return jnp.clip(drawn, min=-reach, max=reach).astype(held_as)


def bell_draw_with(rng, extent, width, reach, cuts, heavy, kind=jnp.bfloat16):
    result = width * jax.random.normal(rng, extent, jnp.float32)
    if cuts:
        result = result * block_levels(rng, extent, cuts, -0.22, 0.18)
    return jnp.clip(with_spikes(result, jax.random.fold_in(rng, 3), *heavy), -reach, reach).astype(kind)


def setup_inputs(seed: int = 0, part: int = 0) -> dict:
    keys = jax.random.split(jax.random.key(seed), 7)
    own_keys = jax.random.split(jax.random.fold_in(keys[6], part), 7)
    return {
        "hidden_input": bell_draw_with(own_keys[0], (TOKENS, MODEL_WIDTH), 1.0, 6.0, ((0, 16),), (0, 1, 16, 2.0)),
        "norm_gain_vector": draw_norm_gain_vector(jax.random.fold_in(keys[6], 71), part),
        "value_matrix": bell_draw(keys[2], (MODEL_WIDTH, KVW), MODEL_WIDTH ** -0.5, 0.0625, ((0, 4),)),
        "adapter_down_map": bell_draw(own_keys[3], (MODEL_WIDTH, ADAPTER_RANK), MODEL_WIDTH ** -0.5, 0.0625, ((0, 4),)),
        "adapter_up_map": draw_adapter_up_map(jax.random.fold_in(jax.random.fold_in(keys[6], part), 71), part),
        "values_gradient": bell_draw(own_keys[5], (TOKENS, KVW), 1.0, 6.0, ((0, 16),)),
    }


norm_eps = 1e-05
adapter_scale = 2.0

def reference(hidden_input, norm_gain_vector, value_matrix, adapter_down_map, adapter_up_map, values_gradient):
    block_rows = math.gcd(TOKENS, 1024)
    num_blocks = TOKENS // block_rows
    stream_all = hidden_input.reshape(num_blocks, block_rows, MODEL_WIDTH)
    values_all = values_gradient.reshape(num_blocks, block_rows, KVW)

    def step_fn(carry, pieces):
        grad_a, gradient_second_map = carry
        stream_blk, values_block = pieces
        stream = stream_blk.astype(jnp.float32)
        inv_rms = lax.rsqrt(lax.optimization_barrier(jnp.mean(stream * stream, axis=1, keepdims=True)) + norm_eps)
        normalized_input = (stream * inv_rms * norm_gain_vector).astype(jnp.bfloat16)
        upward_product = (adapter_scale * jnp.dot(values_block, adapter_up_map.T, preferred_element_type=jnp.float32)).astype(jnp.bfloat16)
        gradient_normalized = (jnp.dot(values_block, value_matrix.T, preferred_element_type=jnp.float32) + jnp.dot(upward_product, adapter_down_map.T, preferred_element_type=jnp.float32)).astype(jnp.bfloat16)
        scaled = gradient_normalized.astype(jnp.float32) * norm_gain_vector
        grad_stream = inv_rms * scaled - stream * (inv_rms ** 3 / MODEL_WIDTH) * lax.optimization_barrier(jnp.sum(scaled * stream, axis=1, keepdims=True))
        latent_code = jnp.dot(normalized_input, adapter_down_map, preferred_element_type=jnp.float32).astype(jnp.bfloat16)
        grad_a = grad_a + jnp.dot(normalized_input.T, upward_product, preferred_element_type=jnp.float32)
        gradient_second_map = gradient_second_map + adapter_scale * jnp.dot(latent_code.T, values_block, preferred_element_type=jnp.float32)
        return ((grad_a, gradient_second_map), grad_stream.astype(jnp.bfloat16))
    start_carry = (jnp.zeros((MODEL_WIDTH, ADAPTER_RANK), jnp.float32), jnp.zeros((ADAPTER_RANK, KVW), jnp.float32))
    (raw_down, raw_up), grad_blocks = lax.scan(step_fn, start_carry, (stream_all, values_all))
    total = jnp.sum(raw_down * raw_down) + jnp.sum(raw_up * raw_up)
    factor = jnp.minimum(1.0, 0.5 * math.sqrt(MODEL_WIDTH * ADAPTER_RANK) / jnp.sqrt(total))
    return (grad_blocks.reshape(TOKENS, MODEL_WIDTH), factor * raw_down, factor * raw_up)
```

```python
import functools
import math

import jax
import jax.numpy as jnp
from jax import lax
from jax.experimental import pallas as pl
from jax.experimental.pallas import tpu as pltpu
from jax.sharding import PartitionSpec as P

norm_eps = 1e-05
adapter_scale = 2.0
MESH = pl.DeviceIdType.MESH
f32, bf16 = jnp.float32, jnp.bfloat16


def dot_nt(a, b):
    return lax.dot_general(a, b, (((1,), (1,)), ((), ())), preferred_element_type=f32)


def dot_tn(a, b):
    return lax.dot_general(a, b, (((0,), (0,)), ((), ())), preferred_element_type=f32)


def kernel(
    n, dp, pair,
    h, gain, w, dt, u, v,
    gh, gd, gu,
    vg, nm, cols, recv, dg, rd_send, rd_recv, rz_send, rz_recv, gd_all,
    pu_send, pu_recv, pz, gu_all, sq,
    v_send, v_sem, c_send, c_sem, da_send, da_sem, db_send, db_sem,
    rd_ssem, rd_rsem, rz_ssem, rz_rsem, gd_ssem, gd_rsem,
    pu_ssem, pu_rsem, pz_ssem, pz_rsem, gu_ssem, gu_rsem, sq_ssem, sq_rsem,
):
    m = dp * pair
    z = lax.axis_index("fsdp")
    p = lax.axis_index("dp") * pair + lax.axis_index("pair")
    tokens, width = h.shape
    features = w.shape[0]
    rank, r = u.shape[0], dt.shape[1]
    tile = min(512, features)

    def at_z(o):
        return {"fsdp": o}

    def at_p(q):
        return {"dp": lax.div(q, pair), "pair": lax.rem(q, pair)}

    def zpeer(d):
        return lax.rem(z + d, n)

    def ppeer(d):
        return lax.rem(p + d, m)

    def remote(src, dst, ssem, rsem, dev):
        return pltpu.make_async_remote_copy(
            src_ref=src, dst_ref=dst, send_sem=ssem, recv_sem=rsem,
            device_id=dev, device_id_type=MESH,
        )

    def each(count, body):
        if count <= 4:
            for d in range(1, count):
                body(d)
        else:
            pl.loop(1, count)(body)

    barrier = pltpu.get_barrier_semaphore()
    each(n, lambda d: pl.semaphore_signal(barrier, inc=1, device_id=at_z(zpeer(d)), device_id_type=MESH))
    each(m, lambda d: pl.semaphore_signal(barrier, inc=1, device_id=at_p(ppeer(d)), device_id_type=MESH))
    pl.semaphore_wait(barrier, n - 1 + m - 1)

    def v_right(src, o, k):
        return remote(src, vg.at[o], v_send.at[0, k], v_sem.at[o], at_z(jnp.minimum(z + 1, n - 1)))

    def v_left(src, o, k):
        return remote(src, vg.at[o], v_send.at[1, k], v_sem.at[o], at_z(jnp.maximum(z - 1, 0)))

    @pl.when(z < n - 1)
    def _():
        v_right(v, z, 0).start()

    @pl.when(z > 0)
    def _():
        v_left(v, z, 0).start()

    def da(d):
        return remote(dt.at[p], dg.at[p, z], da_send.at[d], da_sem.at[z], at_z(zpeer(d)))

    each(n, lambda d: da(d).start())
    dg[p, z] = dt[p]

    def upward_of(block):
        return (adapter_scale * dot_nt(block, u[...])).astype(bf16)

    def tiles(body, init, extent=width):
        def step(i, carry):
            return body(pl.ds(pl.multiple_of(i * tile, tile), tile), i, carry)
        return lax.fori_loop(0, extent // tile, step, init)

    def square(at, i, carry):
        x = h[:, at].astype(f32)
        return carry + jnp.sum(x * x, axis=1, keepdims=True)

    mean = tiles(square, jnp.zeros((tokens, 1), f32)) / width
    inv = lax.rsqrt(mean + norm_eps)
    up_own = upward_of(v[...])
    per = features // tile

    def down_part(at, i, carry):
        x = (h[:, at].astype(f32) * inv * gain[:, at]).astype(bf16)
        nm[:, at] = x
        part = dot_tn(up_own, x).astype(bf16)
        o = lax.div(i, per)
        inner = pl.ds(pl.multiple_of(lax.rem(i, per) * tile, tile), tile)
        for q in range(m):
            rd_send[q, o, :, inner] = part[q * r:(q + 1) * r]
        return carry

    tiles(down_part, 0)

    def rd(d):
        q = ppeer(d)
        return remote(rd_send.at[q], rd_recv.at[p], rd_ssem.at[d], rd_rsem.at[p], at_p(q))

    each(m, lambda d: rd(d).start())

    def columns(block, up, out):
        def step(at, i, carry):
            low = jnp.concatenate([dt[q, :, at] for q in range(m)], axis=0)
            acc = dot_nt(block, w[at, :]) + jnp.dot(up, low, preferred_element_type=f32)
            out[:, at] = acc.astype(bf16)
            return carry
        tiles(step, 0, features)

    def c_copy(o):
        return remote(cols.at[o], recv.at[z], c_send.at[o], c_sem.at[z], at_z(o))

    def c_wait(o):
        remote(cols.at[o], recv.at[o], c_send.at[o], c_sem.at[o], at_z(o)).wait_recv()

    def serve(o):
        block = vg[o]
        columns(block, upward_of(block), cols.at[o])
        c_copy(o).start()

    def v_step(k):
        left, right = z - 1 - k, z + 1 + k

        @pl.when(left >= 0)
        def _():
            v_right(vg.at[left], left, k + 1).wait_recv()

            @pl.when(z < n - 1)
            def _():
                v_right(vg.at[left], left, k + 1).start()

        @pl.when(right < n)
        def _():
            v_left(vg.at[right], right, k + 1).wait_recv()

            @pl.when(z > 0)
            def _():
                v_left(vg.at[right], right, k + 1).start()

        @pl.when(left >= 0)
        def _():
            serve(left)

        @pl.when(right < n)
        def _():
            serve(right)

    v_step(0)

    def da_wait(d):
        o = zpeer(d)
        remote(dt.at[p], dg.at[p, o], da_send.at[d], da_sem.at[o], at_z(o)).wait_recv()

    each(n, da_wait)

    def db(d):
        return remote(dg.at[p], dg.at[p], db_send.at[d], db_sem.at[p], at_p(ppeer(d)))

    each(m, lambda d: db(d).start())

    if n > 2:
        pl.loop(1, n - 1)(v_step)

    columns(v[...], up_own, recv.at[z])

    def rd_wait(d):
        q = ppeer(d)
        remote(rd_send.at[q], rd_recv.at[q], rd_ssem.at[d], rd_rsem.at[q], at_p(q)).wait_recv()

    each(m, rd_wait)

    def rz(d):
        o = zpeer(d)
        return remote(rz_send.at[o], rz_recv.at[z], rz_ssem.at[d], rz_rsem.at[z], at_z(o))

    def reduce_plane(d):
        o = zpeer(d)
        total = rd_send[p, o].astype(f32)
        for e in range(1, m):
            total = total + rd_recv[ppeer(e), o].astype(f32)
        rz_send[o] = total.astype(bf16)
        return total

    def reduce_and_send(d):
        reduce_plane(d)
        rz(d).start()

    each(n, reduce_and_send)
    gd_all[p] = reduce_plane(0)

    def db_wait(d):
        q = ppeer(d)
        remote(dg.at[q], dg.at[q], db_send.at[d], db_sem.at[q], at_p(q)).wait_recv()

    each(m, db_wait)

    def latent_part(at, i, carry):
        o = lax.div(i, per)
        inner = pl.ds(pl.multiple_of(lax.rem(i, per) * tile, tile), tile)
        low = jnp.concatenate([dg[q, o, :, inner] for q in range(m)], axis=0)
        return carry + dot_nt(nm[:, at], low)

    latent = tiles(latent_part, jnp.zeros((tokens, rank), f32)).astype(bf16)
    up_part = adapter_scale * dot_tn(latent, v[...])
    for q in range(m):
        pu_send[q] = up_part[q * r:(q + 1) * r]

    def pu(d):
        q = ppeer(d)
        return remote(pu_send.at[q], pu_recv.at[p], pu_ssem.at[d], pu_rsem.at[p], at_p(q))

    def pu_wait(d):
        q = ppeer(d)
        remote(pu_send.at[q], pu_recv.at[q], pu_ssem.at[d], pu_rsem.at[q], at_p(q)).wait_recv()

    each(m, lambda d: pu(d).start())
    each(m, pu_wait)
    total = pu_send[p]
    for e in range(1, m):
        total = total + pu_recv[ppeer(e)]
    pz[z] = total

    def pz_copy(d):
        return remote(pz.at[z], pz.at[z], pz_ssem.at[d], pz_rsem.at[z], at_z(zpeer(d)))

    def pz_wait(d):
        o = zpeer(d)
        remote(pz.at[o], pz.at[o], pz_ssem.at[d], pz_rsem.at[o], at_z(o)).wait_recv()

    each(n, lambda d: pz_copy(d).start())

    def rz_wait(d):
        o = zpeer(d)
        remote(rz_send.at[o], rz_recv.at[o], rz_ssem.at[d], rz_rsem.at[o], at_z(o)).wait_recv()
        gd_all[p] = gd_all[p] + rz_recv[o].astype(f32)

    each(n, rz_wait)

    def gd_copy(d):
        return remote(gd_all.at[p], gd_all.at[p], gd_ssem.at[d], gd_rsem.at[p], at_p(ppeer(d)))

    def gd_wait(d):
        q = ppeer(d)
        remote(gd_all.at[q], gd_all.at[q], gd_ssem.at[d], gd_rsem.at[q], at_p(q)).wait_recv()

    each(m, lambda d: gd_copy(d).start())
    each(n, pz_wait)
    total = pz[0]
    for o in range(1, n):
        total = total + pz[o]
    gu_all[p] = total

    def gu_copy(d):
        return remote(gu_all.at[p], gu_all.at[p], gu_ssem.at[d], gu_rsem.at[p], at_p(ppeer(d)))

    def gu_wait(d):
        q = ppeer(d)
        remote(gu_all.at[q], gu_all.at[q], gu_ssem.at[d], gu_rsem.at[q], at_p(q)).wait_recv()

    each(m, lambda d: gu_copy(d).start())
    each(m, gd_wait)

    def sum_squares(ref):
        out = jnp.zeros((1, 1), f32)
        for q in range(m):
            x = ref[q]
            x = jnp.sum(x * x, axis=0, keepdims=True)
            out = out + jnp.sum(x, axis=1, keepdims=True)
        return out

    sq[z] = jnp.broadcast_to(sum_squares(gd_all), sq.shape[1:])

    def sq_copy(d):
        return remote(sq.at[z], sq.at[z], sq_ssem.at[d], sq_rsem.at[z], at_z(zpeer(d)))

    def sq_wait(d):
        o = zpeer(d)
        remote(sq.at[o], sq.at[o], sq_ssem.at[d], sq_rsem.at[o], at_z(o)).wait_recv()

    each(n, lambda d: sq_copy(d).start())
    each(m, gu_wait)
    up_squares = sum_squares(gu_all)

    def inner_sum(o, carry):
        def step(at, i, carry):
            whole = pl.ds(pl.multiple_of(o * features + i * tile, tile), tile)
            scaled = recv[o, :, at].astype(f32) * gain[:, whole]
            return carry + jnp.sum(scaled * h[:, whole].astype(f32), axis=1, keepdims=True)
        return tiles(step, carry, features)

    dots = inner_sum(z, jnp.zeros((tokens, 1), f32))

    def arrive(d, dots):
        o = zpeer(d)
        c_wait(o)
        return inner_sum(o, dots)

    dots = lax.fori_loop(1, n, arrive, dots)
    coef = inv * inv * inv / width * dots

    def finish(at, i, carry):
        o = lax.div(i, per)
        inner = pl.ds(pl.multiple_of(lax.rem(i, per) * tile, tile), tile)
        scaled = recv[o, :, inner].astype(f32) * gain[:, at]
        gh[:, at] = (inv * scaled - h[:, at].astype(f32) * coef).astype(bf16)
        return carry

    tiles(finish, 0)

    each(n, sq_wait)
    total = sq[0][:1, :1]
    for o in range(1, n):
        total = total + sq[o][:1, :1]
    total = total + up_squares
    factor = jnp.minimum(1.0, 0.5 * math.sqrt(width * rank) / jnp.sqrt(total))
    for q in range(m):
        gd[q] = factor * gd_all[q]
        gu[q] = factor * gu_all[q]

    @pl.when(z < n - 1)
    def _():
        v_right(v, z, 0).wait_send()

    @pl.when(z > 0)
    def _():
        v_left(v, z, 0).wait_send()

    @pl.loop(0, n - 1)
    def _(k):
        @pl.when((z - 1 - k >= 0) & (z < n - 1))
        def _():
            v_right(v, z, k + 1).wait_send()

        @pl.when((z + 1 + k < n) & (z > 0))
        def _():
            v_left(v, z, k + 1).wait_send()

    def z_sent(d):
        for copy in (da(d), rz(d), pz_copy(d), sq_copy(d), c_copy(zpeer(d))):
            copy.wait_send()

    def p_sent(d):
        for copy in (rd(d), db(d), pu(d), gd_copy(d), gu_copy(d)):
            copy.wait_send()

    each(n, z_sent)
    each(m, p_sent)


def local(n, dp, pair, h, gain, w, d, u, v):
    m = dp * pair
    tokens, width = h.shape
    features, values = w.shape
    rank = u.shape[0]
    r = rank // m
    dt = d.T.reshape(m, r, features)
    vmem = pl.BlockSpec(memory_space=pltpu.VMEM)
    dma = pltpu.SemaphoreType.DMA
    z1, p1 = dma((n,)), dma((m,))
    gh, gd, gu = pl.pallas_call(
        functools.partial(kernel, n, dp, pair),
        out_shape=(
            jax.ShapeDtypeStruct((tokens, width), bf16),
            jax.ShapeDtypeStruct((m, r, features), f32),
            jax.ShapeDtypeStruct((m, r, values), f32),
        ),
        in_specs=[vmem] * 6,
        out_specs=(vmem,) * 3,
        scratch_shapes=[
            pltpu.VMEM((n, tokens, values), bf16),
            pltpu.VMEM((tokens, width), bf16),
            pltpu.VMEM((n, tokens, features), bf16),
            pltpu.VMEM((n, tokens, features), bf16),
            pltpu.VMEM((m, n, r, features), bf16),
            pltpu.VMEM((m, n, r, features), bf16),
            pltpu.VMEM((m, n, r, features), bf16),
            pltpu.VMEM((n, r, features), bf16),
            pltpu.VMEM((n, r, features), bf16),
            pltpu.VMEM((m, r, features), f32),
            pltpu.VMEM((m, r, values), f32),
            pltpu.VMEM((m, r, values), f32),
            pltpu.VMEM((n, r, values), f32),
            pltpu.VMEM((m, r, values), f32),
            pltpu.VMEM((n, 8, 128), f32),
            dma((2, n)), z1, z1, z1, z1, z1, p1, p1,
            p1, p1, z1, z1, p1, p1,
            p1, p1, z1, z1, p1, p1, z1, z1,
        ],
        compiler_params=pltpu.CompilerParams(
            collective_id=0, has_side_effects=True, vmem_limit_bytes=56 * 1024 * 1024
        ),
        name="fused",
    )(h, gain.reshape(1, width), w, dt, u, v)
    return gh, gd.reshape(rank, features).T, gu.reshape(rank, values)


def solution(mesh):
    shape = mesh.shape
    tokens = P(("groups", "fsdp", "dp", "pair"), None)
    return jax.shard_map(
        functools.partial(local, shape["fsdp"], shape["dp"], shape["pair"]),
        mesh=mesh,
        in_specs=(
            tokens, P(), P("fsdp", None), P(("groups", "fsdp"), None), P("groups", None), tokens,
        ),
        out_specs=(tokens, P(("groups", "fsdp"), None), P("groups", None)),
        check_vma=False,
    )
```

```python
import functools
import math

import jax
import jax.numpy as jnp
from jax import lax
from jax.experimental import pallas as pl
from jax.experimental.pallas import tpu as pltpu
from jax.sharding import PartitionSpec as P

norm_eps = 1e-05
adapter_scale = 2.0
MESH = pl.DeviceIdType.MESH
f32, bf16 = jnp.float32, jnp.bfloat16


def dot_nt(a, b):
    return lax.dot_general(a, b, (((1,), (1,)), ((), ())), preferred_element_type=f32)


def dot_tn(a, b):
    return lax.dot_general(a, b, (((0,), (0,)), ((), ())), preferred_element_type=f32)


def kernel(
    n, groups, dp, pair, head,
    h, gain, w, dt, u, v,
    gh, gd, gu,
    vg, nm, ws, cols, cols_head, recv, recv_head, dg, rd_send, rd_recv, rz_send, rz_recv, gd_all,
    pu_send, pu_recv, pz, gu_all, sq,
    v_send, v_sem, w_send, w_sem, s_send, s_sem, f_send, f_sem,
    c_send, c_sem, h_send, h_sem, da_send, da_sem, db_send, db_sem,
    rd_ssem, rd_rsem, rz_ssem, rz_rsem, gd_ssem, gd_rsem,
    pu_ssem, pu_rsem, pz_ssem, pz_rsem, gu_ssem, gu_rsem, sq_ssem, sq_rsem,
):
    m = dp * pair
    z = lax.axis_index("fsdp")
    p = lax.axis_index("dp") * pair + lax.axis_index("pair")
    tokens, width = h.shape
    features = w.shape[0]
    body = features - head
    chips, rows = ws.shape[2], ws.shape[3]
    g, x, c = lax.axis_index("groups"), lax.axis_index("dp"), lax.axis_index("pair")
    chip = g * dp + x
    rank, r = u.shape[0], dt.shape[1]
    tile = min(512, features)

    def at_z(o):
        return {"fsdp": o}

    def at_p(q):
        return {"dp": lax.div(q, pair), "pair": lax.rem(q, pair)}

    def at_chip(d):
        q = lax.rem(chip + d, chips)
        return {"groups": lax.div(q, dp), "dp": lax.rem(q, dp)}

    def at_core(d):
        return {"pair": lax.rem(c + d, pair)}

    def far(o):
        return (o < n // 2) != (z < n // 2)

    def zpeer(d):
        return lax.rem(z + d, n)

    def ppeer(d):
        return lax.rem(p + d, m)

    def remote(src, dst, ssem, rsem, dev):
        return pltpu.make_async_remote_copy(
            src_ref=src, dst_ref=dst, send_sem=ssem, recv_sem=rsem,
            device_id=dev, device_id_type=MESH,
        )

    def each(count, body):
        if count <= 4:
            for d in range(1, count):
                body(d)
        else:
            pl.loop(1, count)(body)

    barrier = pltpu.get_barrier_semaphore()
    each(n, lambda d: pl.semaphore_signal(barrier, inc=1, device_id=at_z(zpeer(d)), device_id_type=MESH))
    each(m, lambda d: pl.semaphore_signal(barrier, inc=1, device_id=at_p(ppeer(d)), device_id_type=MESH))
    others = 0
    if head:
        others = (groups - 1) * dp
        for d in range(1, groups):
            for e in range(dp):
                pl.semaphore_signal(
                    barrier, inc=1, device_id_type=MESH,
                    device_id={"groups": lax.rem(g + d, groups), "dp": lax.rem(x + e, dp)},
                )
    pl.semaphore_wait(barrier, n - 1 + m - 1 + others)

    own_w = w.at[pl.ds(pl.multiple_of((c * chips + chip) * rows, rows), rows)]

    def relay(kind, side, k, o, own=False):
        device = at_z(jnp.minimum(z + 1, n - 1) if side == 0 else jnp.maximum(z - 1, 0))
        if kind == "v":
            dst, ssem, rsem, mine = vg.at[o], v_send, v_sem, v
        elif kind == "d":
            dst, ssem, rsem, mine = dg.at[p, o], da_send, da_sem, dt.at[p]
        else:
            dst, ssem, rsem, mine = ws.at[o, c, chip], w_send, w_sem, own_w
        return remote(mine if own else dst, dst, ssem.at[side, k], rsem.at[o], device)

    kinds = ("v", "d", "w") if head else ("v", "d")

    @pl.when(z < n - 1)
    def _():
        relay("v", 0, 0, z, True).start()

    @pl.when(z > 0)
    def _():
        relay("v", 1, 0, z, True).start()

    for kind in kinds[1:]:
        @pl.when(z < n - 1)
        def _():
            relay(kind, 0, 0, z, True).start()

        @pl.when(z > 0)
        def _():
            relay(kind, 1, 0, z, True).start()

    dg[p, z] = dt[p]

    def upward_of(block):
        return (adapter_scale * dot_nt(block, u[...])).astype(bf16)

    def tiles(body, init, extent=width):
        def step(i, carry):
            return body(pl.ds(pl.multiple_of(i * tile, tile), tile), i, carry)
        return lax.fori_loop(0, extent // tile, step, init)

    def square(at, i, carry):
        x = h[:, at].astype(f32)
        return carry + jnp.sum(x * x, axis=1, keepdims=True)

    mean = tiles(square, jnp.zeros((tokens, 1), f32)) / width
    inv = lax.rsqrt(mean + norm_eps)
    up_own = upward_of(v[...])
    per = features // tile

    def down_part(at, i, carry):
        x = (h[:, at].astype(f32) * inv * gain[:, at]).astype(bf16)
        nm[:, at] = x
        part = dot_tn(up_own, x).astype(bf16)
        o = lax.div(i, per)
        inner = pl.ds(pl.multiple_of(lax.rem(i, per) * tile, tile), tile)
        for q in range(m):
            rd_send[q, o, :, inner] = part[q * r:(q + 1) * r]
        return carry

    tiles(down_part, 0)

    def rd(d):
        q = ppeer(d)
        return remote(rd_send.at[q], rd_recv.at[p], rd_ssem.at[d], rd_rsem.at[p], at_p(q))

    each(m, lambda d: rd(d).start())

    def columns(block, up, out, start, extent):
        width_of = min(tile, extent)

        def step(i, carry):
            to = pl.ds(pl.multiple_of(i * width_of, width_of), width_of)
            at = pl.ds(pl.multiple_of(start + i * width_of, width_of), width_of)
            low = jnp.concatenate([dt[q, :, at] for q in range(m)], axis=0)
            acc = dot_nt(block, w[at, :]) + jnp.dot(up, low, preferred_element_type=f32)
            out[:, to] = acc.astype(bf16)
            return carry
        lax.fori_loop(0, extent // width_of, step, 0)

    def c_copy(o, slot):
        return remote(cols.at[o], recv.at[slot], c_send.at[o], c_sem.at[slot], at_z(o))

    def h_copy(o, slot):
        return remote(
            cols_head.at[o], recv_head.at[slot], h_send.at[o], h_sem.at[slot], at_z(o)
        )

    def serve(o):
        block = vg[o]
        up = upward_of(block)
        columns(block, up, cols.at[o], head, body)
        c_copy(o, z).start()
        if head:
            @pl.when(jnp.logical_not(far(o)))
            def _():
                columns(block, up, cols_head.at[o], 0, head)
                h_copy(o, z).start()

    def share(o, d):
        return remote(
            ws.at[o, c, chip], ws.at[o, c, chip], s_send.at[o, d], s_sem.at[o, chip], at_chip(d)
        )

    def share_wait(o, d):
        q = lax.rem(chip + d, chips)
        remote(
            ws.at[o, c, q], ws.at[o, c, q], s_send.at[o, d], s_sem.at[o, q], at_chip(d)
        ).wait_recv()

    def pass_on(o, d, core):
        return remote(
            ws.at[o, core], ws.at[o, core], f_send.at[o, d], f_sem.at[o, core], at_core(d)
        )

    def each_far(fn):
        @pl.loop(0, n)
        def _(o):
            @pl.when(far(o))
            def _():
                fn(o)

    def take(kind, side, k, o):
        relay(kind, side, k, o).wait_recv()

        @pl.when((z < n - 1) if side == 0 else (z > 0))
        def _():
            relay(kind, side, k, o).start()

    def v_step(k):
        left, right = z - 1 - k, z + 1 + k

        def both(fn):
            @pl.when(left >= 0)
            def _():
                fn(0, left)

            @pl.when(right < n)
            def _():
                fn(1, right)

        both(lambda side, o: take("v", side, k + 1, o))
        both(lambda side, o: serve(o))

        def weights(side, o):
            for kind in kinds[1:]:
                take(kind, side, k + 1, o)
            if head:
                @pl.when(far(o))
                def _():
                    for d in range(1, chips):
                        share(o, d).start()

        both(weights)

    pl.loop(0, n - 1)(v_step)

    def db(d):
        return remote(dg.at[p], dg.at[p], db_send.at[d], db_sem.at[p], at_p(ppeer(d)))

    each(m, lambda d: db(d).start())
    columns(v[...], up_own, recv.at[z], head, body)
    if head:
        columns(v[...], up_own, recv_head.at[z], 0, head)

    def rd_wait(d):
        q = ppeer(d)
        remote(rd_send.at[q], rd_recv.at[q], rd_ssem.at[d], rd_rsem.at[q], at_p(q)).wait_recv()

    each(m, rd_wait)

    def rz(d):
        o = zpeer(d)
        return remote(rz_send.at[o], rz_recv.at[z], rz_ssem.at[d], rz_rsem.at[z], at_z(o))

    def reduce_plane(d):
        o = zpeer(d)
        total = rd_send[p, o].astype(f32)
        for e in range(1, m):
            total = total + rd_recv[ppeer(e), o].astype(f32)
        rz_send[o] = total.astype(bf16)
        return total

    def reduce_and_send(d):
        reduce_plane(d)
        rz(d).start()

    each(n, reduce_and_send)
    gd_all[p] = reduce_plane(0)

    if head:
        def gather(o):
            for d in range(1, chips):
                share_wait(o, d)
            for d in range(1, pair):
                pass_on(o, d, c).start()

        each_far(gather)

    def db_wait(d):
        q = ppeer(d)
        remote(dg.at[q], dg.at[q], db_send.at[d], db_sem.at[q], at_p(q)).wait_recv()

    each(m, db_wait)

    def latent_part(at, i, carry):
        o = lax.div(i, per)
        inner = pl.ds(pl.multiple_of(lax.rem(i, per) * tile, tile), tile)
        low = jnp.concatenate([dg[q, o, :, inner] for q in range(m)], axis=0)
        return carry + dot_nt(nm[:, at], low)

    latent = tiles(latent_part, jnp.zeros((tokens, rank), f32)).astype(bf16)
    up_part = adapter_scale * dot_tn(latent, v[...])
    for q in range(m):
        pu_send[q] = up_part[q * r:(q + 1) * r]

    def pu(d):
        q = ppeer(d)
        return remote(pu_send.at[q], pu_recv.at[p], pu_ssem.at[d], pu_rsem.at[p], at_p(q))

    def pu_wait(d):
        q = ppeer(d)
        remote(pu_send.at[q], pu_recv.at[q], pu_ssem.at[d], pu_rsem.at[q], at_p(q)).wait_recv()

    each(m, lambda d: pu(d).start())
    each(m, pu_wait)
    total = pu_send[p]
    for e in range(1, m):
        total = total + pu_recv[ppeer(e)]
    pz[z] = total.astype(bf16)

    def pz_copy(d):
        return remote(pz.at[z], pz.at[z], pz_ssem.at[d], pz_rsem.at[z], at_z(zpeer(d)))

    def pz_wait(d):
        o = zpeer(d)
        remote(pz.at[o], pz.at[o], pz_ssem.at[d], pz_rsem.at[o], at_z(o)).wait_recv()

    each(n, lambda d: pz_copy(d).start())

    def rz_wait(d):
        o = zpeer(d)
        remote(rz_send.at[o], rz_recv.at[o], rz_ssem.at[d], rz_rsem.at[o], at_z(o)).wait_recv()
        gd_all[p] = gd_all[p] + rz_recv[o].astype(f32)

    each(n, rz_wait)

    def gd_copy(d):
        return remote(gd_all.at[p], gd_all.at[p], gd_ssem.at[d], gd_rsem.at[p], at_p(ppeer(d)))

    def gd_wait(d):
        q = ppeer(d)
        remote(gd_all.at[q], gd_all.at[q], gd_ssem.at[d], gd_rsem.at[q], at_p(q)).wait_recv()

    each(m, lambda d: gd_copy(d).start())
    each(n, pz_wait)
    total = pz[0].astype(f32)
    for o in range(1, n):
        total = total + pz[o].astype(f32)
    gu_all[p] = total

    def gu_copy(d):
        return remote(gu_all.at[p], gu_all.at[p], gu_ssem.at[d], gu_rsem.at[p], at_p(ppeer(d)))

    def gu_wait(d):
        q = ppeer(d)
        remote(gu_all.at[q], gu_all.at[q], gu_ssem.at[d], gu_rsem.at[q], at_p(q)).wait_recv()

    each(m, lambda d: gu_copy(d).start())
    each(m, gd_wait)

    def sum_squares(ref):
        out = jnp.zeros((1, 1), f32)
        for q in range(m):
            x = ref[q]
            x = jnp.sum(x * x, axis=0, keepdims=True)
            out = out + jnp.sum(x, axis=1, keepdims=True)
        return out

    sq[z] = jnp.broadcast_to(sum_squares(gd_all), sq.shape[1:])

    def sq_copy(d):
        return remote(sq.at[z], sq.at[z], sq_ssem.at[d], sq_rsem.at[z], at_z(zpeer(d)))

    def sq_wait(d):
        o = zpeer(d)
        remote(sq.at[o], sq.at[o], sq_ssem.at[d], sq_rsem.at[o], at_z(o)).wait_recv()

    each(n, lambda d: sq_copy(d).start())
    each(m, gu_wait)
    up_squares = sum_squares(gu_all)

    if head:
        def own_head(o):
            for d in range(1, pair):
                pass_on(o, d, lax.rem(c + d, pair)).wait_recv()
            for e in range(pair):
                size = chips * rows
                at = slice(e * size, (e + 1) * size)
                low = jnp.concatenate([dg[q, o, :, at] for q in range(m)], axis=0)
                acc = dot_nt(v[...], ws[o, e].reshape(size, v.shape[1]))
                acc = acc + jnp.dot(up_own, low, preferred_element_type=f32)
                recv_head[o, :, at] = acc.astype(bf16)

        each_far(own_head)

    def sweep(o, source, start, extent, carry, body_of):
        size = min(tile, extent)

        def step(i, carry):
            at = pl.ds(pl.multiple_of(o * features + start + i * size, size), size)
            scaled = source[o, :, pl.ds(pl.multiple_of(i * size, size), size)].astype(f32) * gain[:, at]
            return body_of(scaled, at, carry)
        return lax.fori_loop(0, extent // size, step, carry)

    def both_parts(o, carry, body_of):
        if head:
            carry = sweep(o, recv_head, 0, head, carry, body_of)
        return sweep(o, recv, head, body, carry, body_of)

    def inner_sum(o, carry):
        return both_parts(o, carry, lambda scaled, at, total: total + jnp.sum(
            scaled * h[:, at].astype(f32), axis=1, keepdims=True))

    dots = inner_sum(z, jnp.zeros((tokens, 1), f32))

    def arrive(d, dots):
        o = zpeer(d)
        c_copy(o, o).wait_recv()
        if head:
            @pl.when(jnp.logical_not(far(o)))
            def _():
                h_copy(o, o).wait_recv()
        return inner_sum(o, dots)

    dots = lax.fori_loop(1, n, arrive, dots)
    coef = inv * inv * inv / width * dots

    def finish(scaled, at, carry):
        gh[:, at] = (inv * scaled - h[:, at].astype(f32) * coef).astype(bf16)
        return carry

    lax.fori_loop(0, n, lambda o, carry: both_parts(o, carry, finish), 0)

    each(n, sq_wait)
    total = sq[0][:1, :1]
    for o in range(1, n):
        total = total + sq[o][:1, :1]
    total = total + up_squares
    factor = jnp.minimum(1.0, 0.5 * math.sqrt(width * rank) / jnp.sqrt(total))
    for q in range(m):
        gd[q] = factor * gd_all[q]
        gu[q] = factor * gu_all[q]

    def sent(side, k, o):
        for kind in kinds:
            relay(kind, side, k, o).wait_send()

    @pl.when(z < n - 1)
    def _():
        sent(0, 0, z)

    @pl.when(z > 0)
    def _():
        sent(1, 0, z)

    @pl.loop(0, n - 1)
    def _(k):
        @pl.when((z - 1 - k >= 0) & (z < n - 1))
        def _():
            sent(0, k + 1, z)

        @pl.when((z + 1 + k < n) & (z > 0))
        def _():
            sent(1, k + 1, z)

    def z_sent(d):
        o = zpeer(d)
        for copy in (rz(d), pz_copy(d), sq_copy(d), c_copy(o, z)):
            copy.wait_send()
        if head:
            @pl.when(jnp.logical_not(far(o)))
            def _():
                h_copy(o, z).wait_send()

    def p_sent(d):
        for copy in (rd(d), db(d), pu(d), gd_copy(d), gu_copy(d)):
            copy.wait_send()

    if head:
        def far_sent(o):
            for d in range(1, chips):
                share(o, d).wait_send()
            for d in range(1, pair):
                pass_on(o, d, c).wait_send()

        each_far(far_sent)

    each(n, z_sent)
    each(m, p_sent)


def local(n, groups, dp, pair, h, gain, w, d, u, v):
    m = dp * pair
    tokens, width = h.shape
    features, values = w.shape
    rank = u.shape[0]
    r = rank // m
    slices = groups * m
    head = features // 2 if (features // 2) % (slices * 128) == 0 else 0
    rows = max(head // slices, 16)
    kept = max(head, 128)
    dt = d.T.reshape(m, r, features)
    vmem = pl.BlockSpec(memory_space=pltpu.VMEM)
    dma = pltpu.SemaphoreType.DMA
    z1, p1 = dma((n,)), dma((m,))
    gh, gd, gu = pl.pallas_call(
        functools.partial(kernel, n, groups, dp, pair, head),
        out_shape=(
            jax.ShapeDtypeStruct((tokens, width), bf16),
            jax.ShapeDtypeStruct((m, r, features), f32),
            jax.ShapeDtypeStruct((m, r, values), f32),
        ),
        in_specs=[vmem] * 6,
        out_specs=(vmem,) * 3,
        scratch_shapes=[
            pltpu.VMEM((n, tokens, values), bf16),
            pltpu.VMEM((tokens, width), bf16),
            pltpu.VMEM((n, pair, groups * dp, rows, values), bf16),
            pltpu.VMEM((n, tokens, features - head), bf16),
            pltpu.VMEM((n, tokens, kept), bf16),
            pltpu.VMEM((n, tokens, features - head), bf16),
            pltpu.VMEM((n, tokens, kept), bf16),
            pltpu.VMEM((m, n, r, features), bf16),
            pltpu.VMEM((m, n, r, features), bf16),
            pltpu.VMEM((m, n, r, features), bf16),
            pltpu.VMEM((n, r, features), bf16),
            pltpu.VMEM((n, r, features), bf16),
            pltpu.VMEM((m, r, features), f32),
            pltpu.VMEM((m, r, values), f32),
            pltpu.VMEM((m, r, values), f32),
            pltpu.VMEM((n, r, values), bf16),
            pltpu.VMEM((m, r, values), f32),
            pltpu.VMEM((n, 8, 128), f32),
            dma((2, n)), z1, dma((2, n)), z1,
            dma((n, groups * dp)), dma((n, groups * dp)), dma((n, pair)), dma((n, pair)),
            z1, z1, z1, z1, dma((2, n)), z1, p1, p1,
            p1, p1, z1, z1, p1, p1,
            p1, p1, z1, z1, p1, p1, z1, z1,
        ],
        compiler_params=pltpu.CompilerParams(
            collective_id=0, has_side_effects=True, vmem_limit_bytes=56 * 1024 * 1024
        ),
        name="fused",
    )(h, gain.reshape(1, width), w, dt, u, v)
    return gh, gd.reshape(rank, features).T, gu.reshape(rank, values)


def solution(mesh):
    shape = mesh.shape
    tokens = P(("groups", "fsdp", "dp", "pair"), None)
    return jax.shard_map(
        functools.partial(local, shape["fsdp"], shape["groups"], shape["dp"], shape["pair"]),
        mesh=mesh,
        in_specs=(
            tokens, P(), P("fsdp", None), P(("groups", "fsdp"), None), P("groups", None), tokens,
        ),
        out_specs=(tokens, P(("groups", "fsdp"), None), P("groups", None)),
        check_vma=False,
    )
```

```python
import functools
import math

import jax
import jax.numpy as jnp
from jax import lax
from jax.experimental import pallas as pl
from jax.experimental.pallas import tpu as pltpu
from jax.sharding import PartitionSpec as P

norm_eps = 1e-05
adapter_scale = 2.0
MESH = pl.DeviceIdType.MESH
f32, bf16 = jnp.float32, jnp.bfloat16


def dot_nt(a, b):
    return lax.dot_general(a, b, (((1,), (1,)), ((), ())), preferred_element_type=f32)


def dot_tn(a, b):
    return lax.dot_general(a, b, (((0,), (0,)), ((), ())), preferred_element_type=f32)


def kernel(
    n, groups, dp, pair, head,
    h, gain, w, dt, u, v,
    gh, gd, gu,
    vg, nm, ws, cols, cols_head, recv, recv_head, dg, rd_send, rd_recv, rz_send, rz_recv, gd_all,
    pu_send, pu_recv, pz, gu_all, sq,
    v_send, v_sem, w_send, w_sem, s_send, s_sem, f_send, f_sem,
    c_send, c_sem, h_send, h_sem, da_send, da_sem, db_send, db_sem,
    rd_ssem, rd_rsem, rz_ssem, rz_rsem, gd_ssem, gd_rsem,
    pu_ssem, pu_rsem, pz_ssem, pz_rsem, gu_ssem, gu_rsem, sq_ssem, sq_rsem,
):
    m = dp * pair
    z = lax.axis_index("fsdp")
    p = lax.axis_index("dp") * pair + lax.axis_index("pair")
    tokens, width = h.shape
    features = w.shape[0]
    body = features - head
    chips, rows = ws.shape[2], ws.shape[3]
    g, x, c = lax.axis_index("groups"), lax.axis_index("dp"), lax.axis_index("pair")
    chip = g * dp + x
    rank, r = u.shape[0], dt.shape[1]
    tile = min(512, features)

    def at_z(o):
        return {"fsdp": o}

    def at_p(q):
        return {"dp": lax.div(q, pair), "pair": lax.rem(q, pair)}

    def at_chip(d):
        q = lax.rem(chip + d, chips)
        return {"groups": lax.div(q, dp), "dp": lax.rem(q, dp)}

    def at_core(d):
        return {"pair": lax.rem(c + d, pair)}

    def far(o):
        return (o < n // 2) != (z < n // 2)

    def zpeer(d):
        return lax.rem(z + d, n)

    def ppeer(d):
        return lax.rem(p + d, m)

    def remote(src, dst, ssem, rsem, dev):
        return pltpu.make_async_remote_copy(
            src_ref=src, dst_ref=dst, send_sem=ssem, recv_sem=rsem,
            device_id=dev, device_id_type=MESH,
        )

    def each(count, body):
        if count <= 4:
            for d in range(1, count):
                body(d)
        else:
            pl.loop(1, count)(body)

    barrier = pltpu.get_barrier_semaphore()
    each(n, lambda d: pl.semaphore_signal(barrier, inc=1, device_id=at_z(zpeer(d)), device_id_type=MESH))
    each(m, lambda d: pl.semaphore_signal(barrier, inc=1, device_id=at_p(ppeer(d)), device_id_type=MESH))
    others = 0
    if head:
        others = (groups - 1) * dp
        for d in range(1, groups):
            for e in range(dp):
                pl.semaphore_signal(
                    barrier, inc=1, device_id_type=MESH,
                    device_id={"groups": lax.rem(g + d, groups), "dp": lax.rem(x + e, dp)},
                )
    pl.semaphore_wait(barrier, n - 1 + m - 1 + others)

    own_w = w.at[pl.ds(pl.multiple_of((c * chips + chip) * rows, rows), rows)]

    def relay(kind, side, k, o, own=False):
        device = at_z(jnp.minimum(z + 1, n - 1) if side == 0 else jnp.maximum(z - 1, 0))
        if kind == "v":
            dst, ssem, rsem, mine = vg.at[o], v_send, v_sem, v
        elif kind == "d":
            dst, ssem, rsem, mine = dg.at[p, o], da_send, da_sem, dt.at[p]
        else:
            dst, ssem, rsem, mine = ws.at[o, c, chip], w_send, w_sem, own_w
        return remote(mine if own else dst, dst, ssem.at[side, k], rsem.at[o], device)

    kinds = ("v", "d", "w") if head else ("v", "d")

    @pl.when(z < n - 1)
    def _():
        relay("v", 0, 0, z, True).start()

    @pl.when(z > 0)
    def _():
        relay("v", 1, 0, z, True).start()

    for kind in kinds[1:]:
        @pl.when(z < n - 1)
        def _():
            relay(kind, 0, 0, z, True).start()

        @pl.when(z > 0)
        def _():
            relay(kind, 1, 0, z, True).start()

    dg[p, z] = dt[p]

    def upward_of(block):
        return (adapter_scale * dot_nt(block, u[...])).astype(bf16)

    def tiles(body, init, extent=width):
        def step(i, carry):
            return body(pl.ds(pl.multiple_of(i * tile, tile), tile), i, carry)
        return lax.fori_loop(0, extent // tile, step, init)

    def square(at, i, carry):
        x = h[:, at].astype(f32)
        return carry + jnp.sum(x * x, axis=1, keepdims=True)

    mean = tiles(square, jnp.zeros((tokens, 1), f32)) / width
    inv = lax.rsqrt(mean + norm_eps)
    up_own = upward_of(v[...])
    per = features // tile

    def down_part(at, i, carry):
        x = (h[:, at].astype(f32) * inv * gain[:, at]).astype(bf16)
        nm[:, at] = x
        part = dot_tn(up_own, x).astype(bf16)
        o = lax.div(i, per)
        inner = pl.ds(pl.multiple_of(lax.rem(i, per) * tile, tile), tile)
        for q in range(m):
            rd_send[q, o, :, inner] = part[q * r:(q + 1) * r]
        return carry

    tiles(down_part, 0)

    def rd(d):
        q = ppeer(d)
        return remote(rd_send.at[q], rd_recv.at[p], rd_ssem.at[d], rd_rsem.at[p], at_p(q))

    each(m, lambda d: rd(d).start())

    def columns(block, up, out, start, extent):
        width_of = min(tile, extent)

        def step(i, carry):
            to = pl.ds(pl.multiple_of(i * width_of, width_of), width_of)
            at = pl.ds(pl.multiple_of(start + i * width_of, width_of), width_of)
            low = jnp.concatenate([dt[q, :, at] for q in range(m)], axis=0)
            acc = dot_nt(block, w[at, :]) + jnp.dot(up, low, preferred_element_type=f32)
            out[:, to] = acc.astype(bf16)
            return carry
        lax.fori_loop(0, extent // width_of, step, 0)

    def c_copy(o, slot):
        return remote(cols.at[o], recv.at[slot], c_send.at[o], c_sem.at[slot], at_z(o))

    def h_copy(o, slot):
        return remote(
            cols_head.at[o], recv_head.at[slot], h_send.at[o], h_sem.at[slot], at_z(o)
        )

    def serve(o):
        block = vg[o]
        up = upward_of(block)
        columns(block, up, cols.at[o], head, body)
        c_copy(o, z).start()
        if head:
            @pl.when(jnp.logical_not(far(o)))
            def _():
                columns(block, up, cols_head.at[o], 0, head)
                h_copy(o, z).start()

    def share(o, d):
        return remote(
            ws.at[o, c, chip], ws.at[o, c, chip], s_send.at[o, d], s_sem.at[o, chip], at_chip(d)
        )

    def share_wait(o, d):
        q = lax.rem(chip + d, chips)
        remote(
            ws.at[o, c, q], ws.at[o, c, q], s_send.at[o, d], s_sem.at[o, q], at_chip(d)
        ).wait_recv()

    def pass_on(o, d, core):
        return remote(
            ws.at[o, core], ws.at[o, core], f_send.at[o, d], f_sem.at[o, core], at_core(d)
        )

    def each_far(fn):
        @pl.loop(0, n)
        def _(o):
            @pl.when(far(o))
            def _():
                fn(o)

    def take(kind, side, k, o):
        relay(kind, side, k, o).wait_recv()

        @pl.when((z < n - 1) if side == 0 else (z > 0))
        def _():
            relay(kind, side, k, o).start()

    def both(k, fn):
        left, right = z - 1 - k, z + 1 + k

        @pl.when(left >= 0)
        def _():
            fn(0, left)

        @pl.when(right < n)
        def _():
            fn(1, right)

    def relay_step(k):
        both(k, lambda side, o: take("v", side, k + 1, o))
        both(k, lambda side, o: take("d", side, k + 1, o))
        if head:
            both(k, lambda side, o: take("w", side, k + 1, o))

            def spread(side, o):
                @pl.when(far(o))
                def _():
                    for d in range(1, chips):
                        share(o, d).start()

            both(k, spread)

    def serve_step(k):
        both(k, lambda side, o: serve(o))

    pl.loop(0, n - 1)(relay_step)

    def db(d):
        return remote(dg.at[p], dg.at[p], db_send.at[d], db_sem.at[p], at_p(ppeer(d)))

    each(m, lambda d: db(d).start())
    pl.loop(0, n - 1)(serve_step)

    def rd_wait(d):
        q = ppeer(d)
        remote(rd_send.at[q], rd_recv.at[q], rd_ssem.at[d], rd_rsem.at[q], at_p(q)).wait_recv()

    each(m, rd_wait)

    def rz(d):
        o = zpeer(d)
        return remote(rz_send.at[o], rz_recv.at[z], rz_ssem.at[d], rz_rsem.at[z], at_z(o))

    def reduce_plane(d):
        o = zpeer(d)
        total = rd_send[p, o].astype(f32)
        for e in range(1, m):
            total = total + rd_recv[ppeer(e), o].astype(f32)
        rz_send[o] = total.astype(bf16)
        return total

    def reduce_and_send(d):
        reduce_plane(d)
        rz(d).start()

    each(n, reduce_and_send)
    gd_all[p] = reduce_plane(0)

    if head:
        def gather(o):
            for d in range(1, chips):
                share_wait(o, d)
            for d in range(1, pair):
                pass_on(o, d, c).start()

        each_far(gather)

    columns(v[...], up_own, recv.at[z], head, body)
    if head:
        columns(v[...], up_own, recv_head.at[z], 0, head)

    def db_wait(d):
        q = ppeer(d)
        remote(dg.at[q], dg.at[q], db_send.at[d], db_sem.at[q], at_p(q)).wait_recv()

    each(m, db_wait)

    def latent_part(at, i, carry):
        o = lax.div(i, per)
        inner = pl.ds(pl.multiple_of(lax.rem(i, per) * tile, tile), tile)
        low = jnp.concatenate([dg[q, o, :, inner] for q in range(m)], axis=0)
        return carry + dot_nt(nm[:, at], low)

    latent = tiles(latent_part, jnp.zeros((tokens, rank), f32)).astype(bf16)
    up_part = adapter_scale * dot_tn(latent, v[...])
    for q in range(m):
        pu_send[q] = up_part[q * r:(q + 1) * r]

    def pu(d):
        q = ppeer(d)
        return remote(pu_send.at[q], pu_recv.at[p], pu_ssem.at[d], pu_rsem.at[p], at_p(q))

    def pu_wait(d):
        q = ppeer(d)
        remote(pu_send.at[q], pu_recv.at[q], pu_ssem.at[d], pu_rsem.at[q], at_p(q)).wait_recv()

    each(m, lambda d: pu(d).start())
    each(m, pu_wait)
    total = pu_send[p]
    for e in range(1, m):
        total = total + pu_recv[ppeer(e)]
    pz[z] = total.astype(bf16)

    def pz_copy(d):
        return remote(pz.at[z], pz.at[z], pz_ssem.at[d], pz_rsem.at[z], at_z(zpeer(d)))

    def pz_wait(d):
        o = zpeer(d)
        remote(pz.at[o], pz.at[o], pz_ssem.at[d], pz_rsem.at[o], at_z(o)).wait_recv()

    each(n, lambda d: pz_copy(d).start())

    def rz_wait(d):
        o = zpeer(d)
        remote(rz_send.at[o], rz_recv.at[o], rz_ssem.at[d], rz_rsem.at[o], at_z(o)).wait_recv()
        gd_all[p] = gd_all[p] + rz_recv[o].astype(f32)

    each(n, rz_wait)

    def gd_copy(d):
        return remote(gd_all.at[p], gd_all.at[p], gd_ssem.at[d], gd_rsem.at[p], at_p(ppeer(d)))

    def gd_wait(d):
        q = ppeer(d)
        remote(gd_all.at[q], gd_all.at[q], gd_ssem.at[d], gd_rsem.at[q], at_p(q)).wait_recv()

    each(m, lambda d: gd_copy(d).start())
    if head:
        def own_head(o):
            for d in range(1, pair):
                pass_on(o, d, lax.rem(c + d, pair)).wait_recv()
            for e in range(pair):
                size = chips * rows
                at = slice(e * size, (e + 1) * size)
                low = jnp.concatenate([dg[q, o, :, at] for q in range(m)], axis=0)
                acc = dot_nt(v[...], ws[o, e].reshape(size, v.shape[1]))
                acc = acc + jnp.dot(up_own, low, preferred_element_type=f32)
                recv_head[o, :, at] = acc.astype(bf16)

        each_far(own_head)

    def sweep(o, source, start, extent, carry, body_of):
        size = min(tile, extent)

        def step(i, carry):
            at = pl.ds(pl.multiple_of(o * features + start + i * size, size), size)
            scaled = source[o, :, pl.ds(pl.multiple_of(i * size, size), size)].astype(f32) * gain[:, at]
            return body_of(scaled, at, carry)
        return lax.fori_loop(0, extent // size, step, carry)

    def both_parts(o, carry, body_of):
        if head:
            carry = sweep(o, recv_head, 0, head, carry, body_of)
        return sweep(o, recv, head, body, carry, body_of)

    def inner_sum(o, carry):
        return both_parts(o, carry, lambda scaled, at, total: total + jnp.sum(
            scaled * h[:, at].astype(f32), axis=1, keepdims=True))

    dots = inner_sum(z, jnp.zeros((tokens, 1), f32))

    def arrive(d, dots):
        o = zpeer(d)
        c_copy(o, o).wait_recv()
        if head:
            @pl.when(jnp.logical_not(far(o)))
            def _():
                h_copy(o, o).wait_recv()
        return inner_sum(o, dots)

    dots = lax.fori_loop(1, n, arrive, dots)
    each(m, gd_wait)

    def sum_squares(ref):
        out = jnp.zeros((1, 1), f32)
        for q in range(m):
            x = ref[q]
            x = jnp.sum(x * x, axis=0, keepdims=True)
            out = out + jnp.sum(x, axis=1, keepdims=True)
        return out

    sq[z] = jnp.broadcast_to(sum_squares(gd_all), sq.shape[1:])

    def sq_copy(d):
        return remote(sq.at[z], sq.at[z], sq_ssem.at[d], sq_rsem.at[z], at_z(zpeer(d)))

    def sq_wait(d):
        o = zpeer(d)
        remote(sq.at[o], sq.at[o], sq_ssem.at[d], sq_rsem.at[o], at_z(o)).wait_recv()

    each(n, lambda d: sq_copy(d).start())

    each(n, pz_wait)
    total = pz[0].astype(f32)
    for o in range(1, n):
        total = total + pz[o].astype(f32)
    gu_all[p] = total

    def gu_copy(d):
        return remote(gu_all.at[p], gu_all.at[p], gu_ssem.at[d], gu_rsem.at[p], at_p(ppeer(d)))

    def gu_wait(d):
        q = ppeer(d)
        remote(gu_all.at[q], gu_all.at[q], gu_ssem.at[d], gu_rsem.at[q], at_p(q)).wait_recv()

    each(m, lambda d: gu_copy(d).start())

    coef = inv * inv * inv / width * dots

    def finish(scaled, at, carry):
        gh[:, at] = (inv * scaled - h[:, at].astype(f32) * coef).astype(bf16)
        return carry

    lax.fori_loop(0, n, lambda o, carry: both_parts(o, carry, finish), 0)

    each(m, gu_wait)
    up_squares = sum_squares(gu_all)

    each(n, sq_wait)
    total = sq[0][:1, :1]
    for o in range(1, n):
        total = total + sq[o][:1, :1]
    total = total + up_squares
    factor = jnp.minimum(1.0, 0.5 * math.sqrt(width * rank) / jnp.sqrt(total))
    for q in range(m):
        gd[q] = factor * gd_all[q]
        gu[q] = factor * gu_all[q]

    def sent(side, k, o):
        for kind in kinds:
            relay(kind, side, k, o).wait_send()

    @pl.when(z < n - 1)
    def _():
        sent(0, 0, z)

    @pl.when(z > 0)
    def _():
        sent(1, 0, z)

    @pl.loop(0, n - 1)
    def _(k):
        @pl.when((z - 1 - k >= 0) & (z < n - 1))
        def _():
            sent(0, k + 1, z)

        @pl.when((z + 1 + k < n) & (z > 0))
        def _():
            sent(1, k + 1, z)

    def z_sent(d):
        o = zpeer(d)
        for copy in (rz(d), pz_copy(d), sq_copy(d), c_copy(o, z)):
            copy.wait_send()
        if head:
            @pl.when(jnp.logical_not(far(o)))
            def _():
                h_copy(o, z).wait_send()

    def p_sent(d):
        for copy in (rd(d), db(d), pu(d), gd_copy(d), gu_copy(d)):
            copy.wait_send()

    if head:
        def far_sent(o):
            for d in range(1, chips):
                share(o, d).wait_send()
            for d in range(1, pair):
                pass_on(o, d, c).wait_send()

        each_far(far_sent)

    each(n, z_sent)
    each(m, p_sent)


def local(n, groups, dp, pair, h, gain, w, d, u, v):
    m = dp * pair
    tokens, width = h.shape
    features, values = w.shape
    rank = u.shape[0]
    r = rank // m
    slices = groups * m
    head = features // 4 if (features // 4) % (slices * 64) == 0 else 0
    rows = max(head // slices, 16)
    kept = max(head, 128)
    dt = d.T.reshape(m, r, features)
    vmem = pl.BlockSpec(memory_space=pltpu.VMEM)
    dma = pltpu.SemaphoreType.DMA
    z1, p1 = dma((n,)), dma((m,))
    gh, gd, gu = pl.pallas_call(
        functools.partial(kernel, n, groups, dp, pair, head),
        out_shape=(
            jax.ShapeDtypeStruct((tokens, width), bf16),
            jax.ShapeDtypeStruct((m, r, features), f32),
            jax.ShapeDtypeStruct((m, r, values), f32),
        ),
        in_specs=[vmem] * 6,
        out_specs=(vmem,) * 3,
        scratch_shapes=[
            pltpu.VMEM((n, tokens, values), bf16),
            pltpu.VMEM((tokens, width), bf16),
            pltpu.VMEM((n, pair, groups * dp, rows, values), bf16),
            pltpu.VMEM((n, tokens, features - head), bf16),
            pltpu.VMEM((n, tokens, kept), bf16),
            pltpu.VMEM((n, tokens, features - head), bf16),
            pltpu.VMEM((n, tokens, kept), bf16),
            pltpu.VMEM((m, n, r, features), bf16),
            pltpu.VMEM((m, n, r, features), bf16),
            pltpu.VMEM((m, n, r, features), bf16),
            pltpu.VMEM((n, r, features), bf16),
            pltpu.VMEM((n, r, features), bf16),
            pltpu.VMEM((m, r, features), f32),
            pltpu.VMEM((m, r, values), f32),
            pltpu.VMEM((m, r, values), f32),
            pltpu.VMEM((n, r, values), bf16),
            pltpu.VMEM((m, r, values), f32),
            pltpu.VMEM((n, 8, 128), f32),
            dma((2, n)), z1, dma((2, n)), z1,
            dma((n, groups * dp)), dma((n, groups * dp)), dma((n, pair)), dma((n, pair)),
            z1, z1, z1, z1, dma((2, n)), z1, p1, p1,
            p1, p1, z1, z1, p1, p1,
            p1, p1, z1, z1, p1, p1, z1, z1,
        ],
        compiler_params=pltpu.CompilerParams(
            collective_id=0, has_side_effects=True, vmem_limit_bytes=56 * 1024 * 1024
        ),
        name="fused",
    )(h, gain.reshape(1, width), w, dt, u, v)
    return gh, gd.reshape(rank, features).T, gu.reshape(rank, values)


def solution(mesh):
    shape = mesh.shape
    tokens = P(("groups", "fsdp", "dp", "pair"), None)
    return jax.shard_map(
        functools.partial(local, shape["fsdp"], shape["groups"], shape["dp"], shape["pair"]),
        mesh=mesh,
        in_specs=(
            tokens, P(), P("fsdp", None), P(("groups", "fsdp"), None), P("groups", None), tokens,
        ),
        out_specs=(tokens, P(("groups", "fsdp"), None), P("groups", None)),
        check_vma=False,
    )
```
